32 devices in a mesh: dp: 4 (over z), row: 2 (over x), col: 4 (over y, core).
Axes of the slice: x: 2, y: 2, z: 4, core: 2. Of those that a mesh axis runs over, the one named last changes fastest.
Arguments:
- tokens: bfloat16 [768, 8192], P('col', ('dp', 'row')), may hold values from -6 to 6
- cotangent: bfloat16 [768, 8192], P('col', ('dp', 'row')), may hold values from -6 to 6
- segments: int32 [16, 512], P(('dp', 'col')), may hold values from 0 to 2, as said below
- first_gain: bfloat16 [2, 768], P(None, 'col'), may hold values from 0.099609375 to 1.8984375
- first_shift: bfloat16 [2, 768], P(None, 'col'), may hold values from -3 to 3
- qkv_weight: bfloat16 [2, 768, 3, 768], P(None, 'col', None, 'row'), may hold values from -0.3125 to 0.3125
- qv_bias: bfloat16 [2, 2, 768], P(None, None, 'row'), may hold values from -3 to 3
- out_weight: bfloat16 [2, 768, 768], P(None, 'col', 'row'), may hold values from -0.875 to 0.875
- out_bias: bfloat16 [2, 768], P(None, 'col'), may hold values from -3 to 3
- second_gain: bfloat16 [2, 768], P(None, 'col'), may hold values from 0.099609375 to 1.8984375
- second_shift: bfloat16 [2, 768], P(None, 'col'), may hold values from -3 to 3
- up_weight: bfloat16 [2, 768, 3072], P(None, 'col', 'row'), may hold values from -0.21875 to 0.21875
- up_bias: bfloat16 [2, 3072], P(None, 'row'), may hold values from -3 to 3
- down_weight: bfloat16 [2, 768, 3072], P(None, 'col', 'row'), may hold values from -0.15625 to 0.15625
- down_bias: bfloat16 [2, 768], P(None, 'col'), may hold values from -3 to 3
Outputs:
- activations: bfloat16 [768, 8192], P('col', ('dp', 'row'))
- input_grad: float32 [768, 8192], P('col', ('dp', 'row'))
- first_gain_grad: float32 [2, 768], P(None, 'col')
- first_shift_grad: float32 [2, 768], P(None, 'col')
- qkv_weight_grad: float32 [2, 768, 3, 768], P(None, 'col', None, 'row')
- qv_bias_grad: float32 [2, 2, 768], P(None, None, 'row')
- out_weight_grad: float32 [2, 768, 768], P(None, 'col', 'row')
- out_bias_grad: float32 [2, 768], P(None, 'col')
- second_gain_grad: float32 [2, 768], P(None, 'col')
- second_shift_grad: float32 [2, 768], P(None, 'col')
- up_weight_grad: float32 [2, 768, 3072], P(None, 'col', 'row')
- up_bias_grad: float32 [2, 3072], P(None, 'row')
- down_weight_grad: float32 [2, 768, 3072], P(None, 'col', 'row')
- down_bias_grad: float32 [2, 768], P(None, 'col')
The draws below stay inside these ranges and needn't reach their ends.
Inputs may be any that keep to these rules, and one draw needn't show every extreme that they name: `segments`: within each row (one sequence) the numbers never fall; equal numbers mark one document; each sequence holds three documents, the first and the last cut at the sequence's ends.
All inputs are finite; a program needn't handle non-finite values.
Results may differ from the reference program's by a relative error of at most 0.02.
Values may be sent and summed in bfloat16 or wider, within the bound.
A program may use at most 192 MiB of HBM per device.

```python
import jax
import jax.numpy as jnp
from jax import lax

D = 768
HEADS = 12
HEAD_DIM = 64
FF = 3072
LAYERS = 2
LEN = 512
SEQ_DEV = 4
TOKENS = 8192
N_DP = 4


def draw_segments(key, part):
    key = jax.random.fold_in(key, 7)
    first_key, width_key = jax.random.split(key)
    sequences = TOKENS // LEN
    starts = jax.random.randint(first_key, (sequences, 1), 1, max(LEN // 8, 2))
    widths = jax.random.randint(width_key, (sequences, 1), LEN * 3 // 8, LEN * 3 // 4)
    position = jnp.arange(LEN, dtype=jnp.int32)[None, :]
    first_cut = (position >= starts).astype(jnp.int32)
    second_cut = (position >= starts + widths).astype(jnp.int32)
    return first_cut + second_cut


def steps_of(key, shape, shards, least, high):
    def one(dim, shards_of):
        steps = jax.random.uniform(jax.random.fold_in(jax.random.fold_in(key, 6), dim), (shards_of,), jnp.float32, least / len(shards), high / len(shards))
        return jnp.repeat(jnp.exp(steps), shape[dim] // shards_of).reshape((-1,) + (1,) * (len(shape) - dim - 1))

    loudness = one(*shards[0])
    for cut in shards[1:]:
        loudness = loudness * one(*cut)
    return loudness


def gaussian(stream_key, shape, deviation, most, cuts=(), kind=jnp.bfloat16):
    level = steps_of(stream_key, shape, cuts, -0.22, 0.18) if cuts else 1.0
    entries = jax.random.normal(stream_key, shape, jnp.float32) * deviation * level
    return jnp.minimum(jnp.maximum(entries, -most), most).astype(kind)


def setup_inputs(seed: int = 0) -> dict:
    key_of = jax.random.split(jax.random.key(seed), 16)
    tokens = gaussian(key_of[0], (D, TOKENS), 1.0, 6.0, ((0, 4), (1, 8)))
    cotangent = gaussian(key_of[1], (D, TOKENS), 1.0, 6.0, ((0, 4), (1, 8)))
    segments = draw_segments(jax.random.fold_in(key_of[15], 71), 0)
    first_gain = jnp.clip(1.0 + 0.18 * jax.random.normal(key_of[3], (LAYERS, D), jnp.float32), 0.099609375, 1.8984375).astype(jnp.bfloat16)
    first_shift = gaussian(key_of[4], (LAYERS, D), 0.3, 3.0, ((1, 4),))
    qkv_weight = gaussian(key_of[5], (LAYERS, D, 3, D), (D // 2) ** -0.5, 0.3125, ((1, 4), (3, 2)))
    qv_bias = gaussian(key_of[6], (LAYERS, 2, D), 0.5, 3.0, ((2, 2),))
    out_weight = gaussian(key_of[7], (LAYERS, D, D), (D // 16) ** -0.5, 0.875, ((1, 4), (2, 2)))
    out_bias = gaussian(key_of[8], (LAYERS, D), 0.5, 3.0, ((1, 4),))
    second_gain = jnp.clip(1.0 + 0.18 * jax.random.normal(key_of[9], (LAYERS, D), jnp.float32), 0.099609375, 1.8984375).astype(jnp.bfloat16)
    second_shift = gaussian(key_of[10], (LAYERS, D), 0.3, 3.0, ((1, 4),))
    up_weight = gaussian(key_of[11], (LAYERS, D, FF), D ** -0.5, 0.21875, ((1, 4), (2, 2)))
    up_bias = gaussian(key_of[12], (LAYERS, FF), 0.5, 3.0, ((1, 2),))
    down_weight = gaussian(key_of[13], (LAYERS, D, FF), (FF // 2) ** -0.5, 0.15625, ((1, 4), (2, 2)))
    down_bias = gaussian(key_of[14], (LAYERS, D), 0.5, 3.0, ((1, 4),))
    return {"tokens": tokens, "cotangent": cotangent, "segments": segments, "first_gain": first_gain, "first_shift": first_shift, "qkv_weight": qkv_weight, "qv_bias": qv_bias, "out_weight": out_weight, "out_bias": out_bias, "second_gain": second_gain, "second_shift": second_shift, "up_weight": up_weight, "up_bias": up_bias, "down_weight": down_weight, "down_bias": down_bias}


EPSILON = 1e-05
NEGATIVE = -1e+30
HIGHEST_MODE = lax.Precision.HIGHEST

@jax.custom_vjp
def low(v):
    return lax.optimization_barrier(v.astype(jnp.bfloat16)).astype(jnp.float32)

@jax.custom_vjp
def low_back(v):
    return v

def low_keep(v):
    return (low(v), None)

def low_pass(kept, grad):
    return (grad,)

def back_keep(v):
    return (v, None)

def back_low(kept, grad):
    return (low(grad),)
low.defvjp(low_keep, low_pass)
low_back.defvjp(back_keep, back_low)

def layer_norm(values_in, gain_vec, shift_vec):
    average = lax.optimization_barrier(jnp.mean(values_in, axis=-1, keepdims=True))
    variance = lax.optimization_barrier(jnp.mean(values_in * values_in, axis=-1, keepdims=True)) - average * average
    return (values_in - average) * lax.rsqrt(variance + EPSILON) * gain_vec + shift_vec

def attend(mixed, document):
    seq_count, length = document.shape
    pieces = mixed.reshape(seq_count, length, 3, HEADS, HEAD_DIM)
    queries = pieces[:, :, 0]
    keys_block = pieces[:, :, 1]
    values_block = pieces[:, :, 2]
    scores = jnp.einsum('bqhd,bkhd->bhqk', queries, keys_block, precision=HIGHEST_MODE) * HEAD_DIM ** (-0.5)
    scores = low_back(scores)
    position = jnp.arange(length)
    causal = (position[:, None] >= position[None, :])[None, None]
    same_doc = document[:, None, :, None] == document[:, None, None, :]
    weights_low = low(jax.nn.softmax(jnp.where(causal & same_doc, scores, NEGATIVE), axis=-1))
    attended = jnp.einsum('bhqk,bkhd->bqhd', weights_low, values_block, precision=HIGHEST_MODE)
    return attended.reshape(seq_count * length, HEADS * HEAD_DIM)

def one_layer(hidden, document, weights):
    gain_one, shift_one, qkv_weight, qv_bias, out_weight, out_bias, gain_two, shift_two, up_weight, up_bias, down_weight, down_bias = weights
    normed = low(layer_norm(hidden, gain_one, shift_one))
    offsets = jnp.stack([qv_bias[0], jnp.zeros_like(qv_bias[0]), qv_bias[1]])
    mixed = jnp.einsum('ti,ijo->tjo', normed, qkv_weight, precision=HIGHEST_MODE) + offsets
    mixed = low(low_back(mixed))
    attended = low(low_back(attend(mixed, document)))
    branch = low_back(jnp.dot(attended, out_weight.T, precision=HIGHEST_MODE, preferred_element_type=jnp.float32) + out_bias)
    middle = hidden + branch
    normed_two = low(layer_norm(middle, gain_two, shift_two))
    upward = low_back(jnp.dot(normed_two, up_weight, precision=HIGHEST_MODE, preferred_element_type=jnp.float32) + up_bias)
    active = low(jax.nn.gelu(upward, approximate=True))
    branch_two = low_back(jnp.dot(active, down_weight.T, precision=HIGHEST_MODE, preferred_element_type=jnp.float32) + down_bias)
    return middle + branch_two

def all_layers(hidden, document, floats):
    for level in range(LAYERS):
        hidden = one_layer(hidden, document, tuple((member[level] for member in floats)))
    return hidden

def reference(tokens, cotangent, segments, first_gain, first_shift, qkv_weight, qv_bias, out_weight, out_bias, second_gain, second_shift, up_weight, up_bias, down_weight, down_bias):
    initials = (first_gain, first_shift, qkv_weight, qv_bias, out_weight, out_bias, second_gain, second_shift, up_weight, up_bias, down_weight, down_bias)
    floats = tuple((member.astype(jnp.float32) for member in initials))
    inputs = tokens.astype(jnp.float32).T.reshape(N_DP, SEQ_DEV * LEN, D)
    upstream = cotangent.astype(jnp.float32).T.reshape(N_DP, SEQ_DEV * LEN, D)
    documents = segments.reshape(N_DP, SEQ_DEV, LEN)

    def forward(inputs, floats):
        one_group = jax.checkpoint(lambda hidden, document: all_layers(hidden, document, floats))
        return lax.map(lambda pieces: one_group(pieces[0], pieces[1]), (inputs, documents))
    result, pullback = jax.vjp(forward, inputs, floats)
    grad_inputs, grad_params = pullback(upstream)
    return (result.reshape(TOKENS, D).T.astype(jnp.bfloat16), grad_inputs.reshape(TOKENS, D).T, grad_params[0], grad_params[1], grad_params[2], grad_params[3], grad_params[4], grad_params[5], grad_params[6], grad_params[7], grad_params[8], grad_params[9], grad_params[10], grad_params[11])
```

```python
from functools import partial

import jax
import jax.numpy as jnp
from jax import lax
from jax.sharding import Mesh, PartitionSpec as P

HEAD_DIM = 64
EPSILON = 1e-05
NEGATIVE = -1e30
PLANE = ("row", "pair")


def contract_rows(left_side, right_side):
    return lax.dot_general(
        left_side, right_side, (((0,), (0,)), ((), ())), preferred_element_type=jnp.float32
    )


def contract_cols(left_side, right_side):
    return lax.dot_general(
        left_side, right_side, (((1,), (1,)), ((), ())), preferred_element_type=jnp.float32
    )


def plain(left_side, right_side):
    return jnp.dot(left_side, right_side, preferred_element_type=jnp.float32)


def pair_sum(value):
    return value + lax.ppermute(value, "core", [(0, 1), (1, 0)])


def norm_forward(residual, gain_vec, shift_vec):
    average = jnp.mean(residual, axis=1, keepdims=True)
    variance = jnp.mean(residual * residual, axis=1, keepdims=True) - average * average
    inverse = lax.rsqrt(variance + EPSILON)
    unit_rows = (residual - average) * inverse
    return ((unit_rows * gain_vec + shift_vec).astype(jnp.bfloat16), unit_rows, inverse)


def norm_backward(upstream, unit_rows, inverse, gain_vec):
    scaled = upstream * gain_vec
    first = jnp.mean(scaled, axis=1, keepdims=True)
    second = jnp.mean(scaled * unit_rows, axis=1, keepdims=True)
    result = inverse * (scaled - first - unit_rows * second)
    return (result, jnp.sum(upstream * unit_rows, axis=0), jnp.sum(upstream, axis=0))


def masked_scores(queries, keys_block, document):
    length = document.shape[0]
    position = jnp.arange(length)
    allowed = (position[:, None] >= position[None, :]) & (document[:, None] == document[None, :])
    scores = jnp.einsum(
        "hqd,hkd->hqk", queries, keys_block, preferred_element_type=jnp.float32
    ) * HEAD_DIM ** (-0.5)
    return jnp.where(allowed[None], scores, NEGATIVE)


def by_heads(value):
    return value.reshape(value.shape[0], -1, HEAD_DIM).transpose(1, 0, 2)


def from_heads(value):
    return value.transpose(1, 0, 2).reshape(value.shape[1], -1)


def attend_forward(queries, keys_block, values_block, document):
    scores = masked_scores(queries, keys_block, document)
    highest = jnp.max(scores, axis=-1, keepdims=True)
    exponent = jnp.exp(scores - highest)
    denominator = jnp.sum(exponent, axis=-1, keepdims=True)
    weights_low = (exponent / denominator).astype(jnp.bfloat16)
    attended = jnp.einsum(
        "hqk,hkd->hqd", weights_low, values_block, preferred_element_type=jnp.float32
    )
    return (attended, highest + jnp.log(denominator))


def attend_backward(queries, keys_block, values_block, document, logsum, out_grad):
    factor = HEAD_DIM ** (-0.5)
    probs = jnp.exp(masked_scores(queries, keys_block, document) - logsum)
    value_grad = jnp.einsum(
        "hqk,hqd->hkd", probs.astype(jnp.bfloat16), out_grad, preferred_element_type=jnp.float32
    )
    prob_grad = jnp.einsum(
        "hqd,hkd->hqk", out_grad, values_block, preferred_element_type=jnp.float32
    )
    inner_sum = jnp.sum(probs * prob_grad, axis=-1, keepdims=True)
    score_grad = (probs * (prob_grad - inner_sum)).astype(jnp.bfloat16)
    query_grad = (
        jnp.einsum("hqk,hkd->hqd", score_grad, keys_block, preferred_element_type=jnp.float32)
        * factor
    )
    key_grad = (
        jnp.einsum("hqk,hqd->hkd", score_grad, queries, preferred_element_type=jnp.float32)
        * factor
    )
    return query_grad, key_grad, value_grad


def share_weights(parts):
    joined = jnp.concatenate(parts, axis=-1)
    mine = lax.all_to_all(joined, "core", split_axis=2, concat_axis=1, tiled=True)
    return mine[:, :, 0]


def gather_plane(piece):
    everything = lax.all_gather(piece, PLANE, axis=0, tiled=False)
    rows = lax.axis_size("row")
    return everything.reshape(rows, -1, piece.shape[-1])


def scatter_plane(grads):
    pairs = lax.axis_size("pair")
    stacked = jnp.stack(grads).astype(jnp.bfloat16)
    stacked = stacked.reshape(len(grads) * pairs, -1, stacked.shape[-1])
    return lax.psum_scatter(stacked, PLANE, scatter_dimension=0, tiled=False)


def return_weights(piece):
    depth = piece.shape[0] // 2
    return lax.all_to_all(
        piece.reshape(2, depth, 1, piece.shape[-1]), "core", split_axis=0, concat_axis=2, tiled=True
    )[0].astype(jnp.float32)


def shards(
    tokens,
    cotangent,
    segments,
    first_gain,
    first_shift,
    qkv_weight,
    qv_bias,
    out_weight,
    out_bias,
    second_gain,
    second_shift,
    up_weight,
    up_bias,
    down_weight,
    down_bias,
):
    layers, depth_in, _, head_width = qkv_weight.shape
    hidden_width = up_weight.shape[2]
    half_head, half_hidden = head_width // 2, hidden_width // 2
    rows, pairs = lax.axis_size("row"), lax.axis_size("pair")
    at_row, at_pair, at_core = (lax.axis_index(name) for name in ("row", "pair", "core"))
    width = depth_in * pairs * 2
    length = segments.shape[1]

    attention_part = share_weights(
        [
            qkv_weight.reshape(layers, depth_in, 3, 2, half_head)
            .transpose(0, 1, 3, 2, 4)
            .reshape(layers, depth_in, 2, 3 * half_head),
            out_weight.reshape(layers, depth_in, 2, half_head),
        ]
    )
    forward_part = share_weights(
        [
            up_weight.reshape(layers, depth_in, 2, half_hidden),
            down_weight.reshape(layers, depth_in, 2, half_hidden),
        ]
    )
    attention_weights = []
    forward_weights = []
    for layer_at in range(layers):
        attention_weights.append(gather_plane(attention_part[layer_at]))
        forward_weights.append(gather_plane(forward_part[layer_at]))

    small = jnp.concatenate(
        [
            jnp.stack(
                [first_gain, first_shift, out_bias, second_gain, second_shift, down_bias]
            ).reshape(-1),
            qv_bias.reshape(-1),
            up_bias.reshape(-1),
            segments[0].astype(jnp.bfloat16),
        ]
    )
    small = lax.all_gather(small, ("row", "pair", "core"), axis=0, tiled=False).astype(jnp.float32)
    small = small.reshape(rows, pairs * 2, -1)
    cuts = [6 * layers * depth_in, 2 * layers * head_width, layers * hidden_width]
    cuts = [cuts[0], cuts[0] + cuts[1], cuts[0] + cuts[1] + cuts[2]]
    vectors = small[0, :, : cuts[0]].reshape(pairs * 2, 6, layers, depth_in)
    vectors = vectors.transpose(1, 2, 0, 3).reshape(6, layers, width)
    query_bias = small[:, 0, cuts[0] : cuts[1]].reshape(rows, layers, 2, 2, half_head)
    query_bias = lax.dynamic_index_in_dim(query_bias, at_core, 3, keepdims=False)
    hidden_bias = small[:, 0, cuts[1] : cuts[2]].reshape(rows, layers, 2, half_hidden)
    hidden_bias = lax.dynamic_index_in_dim(hidden_bias, at_core, 2, keepdims=False)
    document = lax.dynamic_index_in_dim(
        small[0, :, cuts[2] :], at_row * pairs + at_pair, 0, keepdims=False
    )

    both = jnp.stack([tokens, cotangent])
    both = lax.all_gather(both, "core", axis=1, tiled=True)
    both = lax.all_to_all(both, "pair", split_axis=2, concat_axis=1, tiled=True)
    residual = both[0].astype(jnp.float32).T
    gradient = both[1].astype(jnp.float32).T

    stored = []
    for layer_at in range(layers):
        gain_one, shift_one, bias_out, gain_two, shift_two, bias_down = vectors[:, layer_at]
        mixing = attention_weights[layer_at]
        normed_one, unit_one, inverse_one = norm_forward(residual, gain_one, shift_one)
        mixed = []
        for row in range(rows):
            offsets = jnp.concatenate(
                [
                    query_bias[row, layer_at, 0],
                    jnp.zeros((half_head,), jnp.float32),
                    query_bias[row, layer_at, 1],
                ]
            )
            produced = plain(normed_one, mixing[row][:, : 3 * half_head]) + offsets
            mixed.append(produced.astype(jnp.bfloat16).reshape(length, 3, half_head))
        mixed = jnp.concatenate(mixed, axis=2)
        heads = [by_heads(mixed[:, part]) for part in range(3)]
        attended, logsum = attend_forward(*heads, document)
        attended_low = from_heads(attended.astype(jnp.bfloat16))
        branch = sum(
            contract_cols(
                attended_low[:, row * half_head : (row + 1) * half_head],
                mixing[row][:, 3 * half_head :],
            )
            for row in range(rows)
        )
        middle = residual + (pair_sum(branch) + bias_out)
        normed_two, unit_two, inverse_two = norm_forward(middle, gain_two, shift_two)
        wide = forward_weights[layer_at]
        upward = [
            plain(normed_two, wide[row][:, :half_hidden]) + hidden_bias[row, layer_at]
            for row in range(rows)
        ]
        active = [jax.nn.gelu(part, approximate=True).astype(jnp.bfloat16) for part in upward]
        branch_two = sum(
            contract_cols(active[row], wide[row][:, half_hidden:]) for row in range(rows)
        )
        stored.append(
            (
                normed_one,
                unit_one,
                inverse_one,
                heads,
                logsum,
                attended_low,
                normed_two,
                unit_two,
                inverse_two,
                upward,
                active,
            )
        )
        residual = middle + (pair_sum(branch_two) + bias_down)

    def to_owner(value):
        blocks = value.T.reshape(pairs, 2, depth_in, length)
        blocks = lax.dynamic_index_in_dim(blocks, at_core, 1, keepdims=False)
        return lax.all_to_all(blocks, "pair", split_axis=0, concat_axis=2, tiled=True)[0]

    activations = to_owner(residual.astype(jnp.bfloat16))

    vector_parts = [None] * layers
    attention_grads = [None] * layers
    forward_grads = [None] * layers
    for layer_at in reversed(range(layers)):
        (
            normed_one,
            unit_one,
            inverse_one,
            heads,
            logsum,
            attended_low,
            normed_two,
            unit_two,
            inverse_two,
            upward,
            active,
        ) = stored[layer_at]
        gain_one, _, _, gain_two, _, _ = vectors[:, layer_at]
        mixing, wide = attention_weights[layer_at], forward_weights[layer_at]
        down_in = gradient.astype(jnp.bfloat16)
        hidden_grads = []
        parts = []
        normed_grad = 0.0
        for row in range(rows):
            down_grad = contract_rows(down_in, active[row])
            active_grad = plain(down_in, wide[row][:, half_hidden:])
            _, gelu_pull = jax.vjp(partial(jax.nn.gelu, approximate=True), upward[row])
            hidden_grad = gelu_pull(active_grad)[0].astype(jnp.bfloat16)
            up_grad = contract_rows(normed_two, hidden_grad)
            normed_grad = normed_grad + contract_cols(hidden_grad, wide[row][:, :half_hidden])
            hidden_grads.append(jnp.sum(hidden_grad.astype(jnp.float32), axis=0))
            parts.append(jnp.concatenate([up_grad, down_grad], axis=1))
        forward_grads[layer_at] = lax.psum(scatter_plane(parts), "dp")
        back_two, gain_two_grad, shift_two_grad = norm_backward(
            pair_sum(normed_grad), unit_two, inverse_two, gain_two
        )
        middle_grad = gradient + back_two
        out_in = middle_grad.astype(jnp.bfloat16)
        out_grads = []
        attended_grad = []
        for row in range(rows):
            span = slice(row * half_head, (row + 1) * half_head)
            out_grads.append(contract_rows(out_in, attended_low[:, span]))
            attended_grad.append(plain(out_in, mixing[row][:, 3 * half_head :]))
        attended_grad = jnp.concatenate(attended_grad, axis=1).astype(jnp.bfloat16)
        mixed_grad = [
            from_heads(part.astype(jnp.bfloat16))
            for part in attend_backward(*heads, document, logsum, by_heads(attended_grad))
        ]
        parts = []
        normed_grad = 0.0
        for row in range(rows):
            span = slice(row * half_head, (row + 1) * half_head)
            pieces = jnp.concatenate([part[:, span] for part in mixed_grad], axis=1)
            parts.append(
                jnp.concatenate([contract_rows(normed_one, pieces), out_grads[row]], axis=1)
            )
            normed_grad = normed_grad + contract_cols(pieces, mixing[row][:, : 3 * half_head])
        attention_grads[layer_at] = lax.psum(scatter_plane(parts), "dp")
        back_one, gain_one_grad, shift_one_grad = norm_backward(
            pair_sum(normed_grad), unit_one, inverse_one, gain_one
        )
        query_sums = jnp.stack(
            [jnp.sum(mixed_grad[part].astype(jnp.float32), axis=0) for part in (0, 2)]
        )
        vector_parts[layer_at] = (
            jnp.stack(
                [
                    gain_one_grad,
                    shift_one_grad,
                    jnp.sum(out_in.astype(jnp.float32), axis=0),
                    gain_two_grad,
                    shift_two_grad,
                    jnp.sum(down_in.astype(jnp.float32), axis=0),
                ]
            ),
            query_sums.reshape(2, rows, half_head),
            jnp.stack(hidden_grads),
        )
        gradient = middle_grad + back_one

    input_grad = to_owner(gradient)
    deep, asked, hidden = (
        jnp.stack([vector_parts[layer_at][part] for layer_at in range(layers)]) for part in range(3)
    )
    sums = lax.psum(
        jnp.concatenate([deep.reshape(-1), asked.reshape(-1), hidden.reshape(-1)]),
        ("dp", "row", "pair"),
    )
    hidden_sums = lax.all_gather(sums[deep.size :], "core", axis=0, tiled=False)
    deep_sums = lax.dynamic_slice_in_dim(
        sums[: deep.size].reshape(layers, 6, width), (at_pair * 2 + at_core) * depth_in, depth_in, 2
    )
    asked_sums = hidden_sums[:, : asked.size].reshape(2, layers, 2, rows, half_head)
    asked_sums = lax.dynamic_index_in_dim(asked_sums, at_row, 3, keepdims=False)
    asked_sums = asked_sums.transpose(1, 2, 0, 3).reshape(layers, 2, head_width)
    up_sums = hidden_sums[:, asked.size :].reshape(2, layers, rows, half_hidden)
    up_sums = lax.dynamic_index_in_dim(up_sums, at_row, 2, keepdims=False)
    up_sums = up_sums.transpose(1, 0, 2).reshape(layers, hidden_width)

    attention_out = jnp.stack([return_weights(part) for part in attention_grads])
    forward_out = jnp.stack([return_weights(part) for part in forward_grads])
    qkv_grad = attention_out[..., : 3 * half_head].reshape(layers, depth_in, 2, 3, half_head)
    qkv_grad = qkv_grad.transpose(0, 1, 3, 2, 4).reshape(layers, depth_in, 3, head_width)
    out_grad = attention_out[..., 3 * half_head :].reshape(layers, depth_in, head_width)
    up_grad = forward_out[..., :half_hidden].reshape(layers, depth_in, hidden_width)
    down_grad = forward_out[..., half_hidden:].reshape(layers, depth_in, hidden_width)
    return (
        activations,
        input_grad,
        deep_sums[:, 0],
        deep_sums[:, 1],
        qkv_grad,
        asked_sums,
        out_grad,
        deep_sums[:, 2],
        deep_sums[:, 3],
        deep_sums[:, 4],
        up_grad,
        up_sums,
        down_grad,
        deep_sums[:, 5],
    )


def solution(mesh):
    devices = mesh.devices
    depth, rows, cols = devices.shape
    chips = Mesh(devices.reshape(depth, rows, cols // 2, 2), ("dp", "row", "pair", "core"))
    col = ("pair", "core")
    placed = (
        P(col, ("dp", "row")),
        P(col, ("dp", "row")),
        P(("dp", "pair", "core"), None),
        P(None, col),
        P(None, col),
        P(None, col, None, "row"),
        P(None, None, "row"),
        P(None, col, "row"),
        P(None, col),
        P(None, col),
        P(None, col),
        P(None, col, "row"),
        P(None, "row"),
        P(None, col, "row"),
        P(None, col),
    )
    return jax.shard_map(
        shards,
        mesh=chips,
        in_specs=placed,
        out_specs=(
            P(col, ("dp", "row")),
            P(col, ("dp", "row")),
            P(None, col),
            P(None, col),
            P(None, col, None, "row"),
            P(None, None, "row"),
            P(None, col, "row"),
            P(None, col),
            P(None, col),
            P(None, col),
            P(None, col, "row"),
            P(None, "row"),
            P(None, col, "row"),
            P(None, col),
        ),
        check_vma=False,
    )
```

```python
from functools import partial

import jax
import jax.numpy as jnp
from jax import lax
from jax.sharding import Mesh, PartitionSpec as P

HEAD_DIM = 64
EPSILON = 1e-05
NEGATIVE = -1e30
PLANE = ("row", "pair")


def contract_rows(left_side, right_side):
    return lax.dot_general(
        left_side, right_side, (((0,), (0,)), ((), ())), preferred_element_type=jnp.float32
    )


def contract_cols(left_side, right_side):
    return lax.dot_general(
        left_side, right_side, (((1,), (1,)), ((), ())), preferred_element_type=jnp.float32
    )


def plain(left_side, right_side):
    return jnp.dot(left_side, right_side, preferred_element_type=jnp.float32)


def pair_sum(value):
    return value + lax.ppermute(value, "core", [(0, 1), (1, 0)])


def norm_forward(residual, gain_vec, shift_vec):
    average = jnp.mean(residual, axis=1, keepdims=True)
    variance = jnp.mean(residual * residual, axis=1, keepdims=True) - average * average
    inverse = lax.rsqrt(variance + EPSILON)
    unit_rows = (residual - average) * inverse
    return ((unit_rows * gain_vec + shift_vec).astype(jnp.bfloat16), unit_rows, inverse)


def norm_backward(upstream, unit_rows, inverse, gain_vec):
    scaled = upstream * gain_vec
    first = jnp.mean(scaled, axis=1, keepdims=True)
    second = jnp.mean(scaled * unit_rows, axis=1, keepdims=True)
    result = inverse * (scaled - first - unit_rows * second)
    return (result, jnp.sum(upstream * unit_rows, axis=0), jnp.sum(upstream, axis=0))


def masked_scores(queries, keys_block, document):
    length = document.shape[0]
    position = jnp.arange(length)
    allowed = (position[:, None] >= position[None, :]) & (document[:, None] == document[None, :])
    scores = jnp.einsum(
        "hqd,hkd->hqk", queries, keys_block, preferred_element_type=jnp.float32
    ) * HEAD_DIM ** (-0.5)
    return jnp.where(allowed[None], scores, NEGATIVE)


def by_heads(value):
    return value.reshape(value.shape[0], -1, HEAD_DIM).transpose(1, 0, 2)


def from_heads(value):
    return value.transpose(1, 0, 2).reshape(value.shape[1], -1)


def attend_forward(queries, keys_block, values_block, document):
    scores = masked_scores(queries, keys_block, document)
    highest = jnp.max(scores, axis=-1, keepdims=True)
    exponent = jnp.exp(scores - highest)
    denominator = jnp.sum(exponent, axis=-1, keepdims=True)
    weights_low = (exponent / denominator).astype(jnp.bfloat16)
    attended = jnp.einsum(
        "hqk,hkd->hqd", weights_low, values_block, preferred_element_type=jnp.float32
    )
    return (attended, highest + jnp.log(denominator))


def attend_backward(queries, keys_block, values_block, document, logsum, out_grad):
    factor = HEAD_DIM ** (-0.5)
    probs = jnp.exp(masked_scores(queries, keys_block, document) - logsum)
    value_grad = jnp.einsum(
        "hqk,hqd->hkd", probs.astype(jnp.bfloat16), out_grad, preferred_element_type=jnp.float32
    )
    prob_grad = jnp.einsum(
        "hqd,hkd->hqk", out_grad, values_block, preferred_element_type=jnp.float32
    )
    inner_sum = jnp.sum(probs * prob_grad, axis=-1, keepdims=True)
    score_grad = (probs * (prob_grad - inner_sum)).astype(jnp.bfloat16)
    query_grad = (
        jnp.einsum("hqk,hkd->hqd", score_grad, keys_block, preferred_element_type=jnp.float32)
        * factor
    )
    key_grad = (
        jnp.einsum("hqk,hqd->hkd", score_grad, queries, preferred_element_type=jnp.float32)
        * factor
    )
    return query_grad, key_grad, value_grad


def swap(value, axis):
    return lax.ppermute(value, axis, [(0, 1), (1, 0)])


def by_core(mine, other, axis):
    first = lax.axis_index("core") == 0
    return jnp.concatenate([jnp.where(first, mine, other), jnp.where(first, other, mine)], axis)


def share_weights(parts):
    joined = jnp.concatenate(parts, axis=-1)
    first = lax.axis_index("core") == 0
    kept = jnp.where(first, joined[:, 0], joined[:, 1])
    given = jnp.where(first, joined[:, 1], joined[:, 0])
    return by_core(kept, swap(given, "core"), 0)


def gather_plane(piece):
    half = piece.shape[0] // 2
    over_row, over_pair = swap(piece, "row"), swap(piece, "pair")
    top, bottom = swap(over_row[:half], "pair"), swap(over_pair[half:], "row")
    return (
        jnp.concatenate([piece, over_pair], axis=0),
        jnp.concatenate([over_row, top, bottom], axis=0),
    )


def added(left_side, right_side):
    return left_side.astype(jnp.float32) + right_side.astype(jnp.float32)


def scatter_plane(grads):
    own, other = (part.astype(jnp.bfloat16).reshape(2, 2, -1, part.shape[-1]) for part in grads)
    sum_top = added(own[:, 0], swap(other[:, 0], "row")).astype(jnp.bfloat16)
    theirs = swap(jnp.stack([own[1, 1], other[1, 1]]), "pair")
    sum_own = added(own[0, 1], theirs[0])
    sum_other = added(other[0, 1], theirs[1]).astype(jnp.bfloat16)
    top = added(sum_top[0], swap(sum_top[1], "pair")).astype(jnp.bfloat16)
    bottom = added(sum_own, swap(sum_other, "row")).astype(jnp.bfloat16)
    return jnp.stack([top, bottom])


def return_weights(piece):
    first = lax.axis_index("core") == 0
    kept = jnp.where(first, piece[0], piece[1])
    given = jnp.where(first, piece[1], piece[0])
    return by_core(kept[:, None], swap(given, "core")[:, None], 1).astype(jnp.float32)


def chained(value, before):
    return lax.optimization_barrier((value, before))[0]


def shards(
    tokens,
    cotangent,
    segments,
    first_gain,
    first_shift,
    qkv_weight,
    qv_bias,
    out_weight,
    out_bias,
    second_gain,
    second_shift,
    up_weight,
    up_bias,
    down_weight,
    down_bias,
):
    layers, depth_in, _, head_width = qkv_weight.shape
    hidden_width = up_weight.shape[2]
    half_head, half_hidden = head_width // 2, hidden_width // 2
    rows, pairs = lax.axis_size("row"), lax.axis_size("pair")
    at_row, at_pair, at_core = (lax.axis_index(name) for name in ("row", "pair", "core"))
    width = depth_in * pairs * 2
    length = segments.shape[1]

    attention_weights = []
    forward_weights = []
    for layer_at in range(layers):
        attention_weights.append(
            gather_plane(
                share_weights(
                    [
                        qkv_weight[layer_at]
                        .reshape(depth_in, 3, 2, half_head)
                        .transpose(0, 2, 1, 3)
                        .reshape(depth_in, 2, 3 * half_head),
                        out_weight[layer_at].reshape(depth_in, 2, half_head),
                    ]
                )
            )
        )
        forward_weights.append(
            gather_plane(
                share_weights(
                    [
                        up_weight[layer_at].reshape(depth_in, 2, half_hidden),
                        down_weight[layer_at].reshape(depth_in, 2, half_hidden),
                    ]
                )
            )
        )

    small = jnp.concatenate(
        [
            jnp.stack(
                [first_gain, first_shift, out_bias, second_gain, second_shift, down_bias]
            ).reshape(-1),
            qv_bias.reshape(-1),
            up_bias.reshape(-1),
            segments[0].astype(jnp.bfloat16),
        ]
    )
    small = lax.all_gather(small, ("row", "pair", "core"), axis=0, tiled=False).astype(jnp.float32)
    small = small.reshape(rows, pairs * 2, -1)
    document = lax.dynamic_index_in_dim(
        small[0, :, small.shape[-1] - length :], at_row * pairs + at_pair, 0, keepdims=False
    )
    small = small.reshape(rows, pairs, 2, -1)
    small = jnp.where(at_row == 0, small, small[::-1])
    small = jnp.where(at_pair == 0, small, small[:, ::-1]).reshape(rows, pairs * 2, -1)
    cuts = [6 * layers * depth_in, 2 * layers * head_width, layers * hidden_width]
    cuts = [cuts[0], cuts[0] + cuts[1], cuts[0] + cuts[1] + cuts[2]]
    vectors = small[0, :, : cuts[0]].reshape(pairs * 2, 6, layers, depth_in)
    vectors = vectors.transpose(1, 2, 0, 3).reshape(6, layers, width)
    query_bias = small[:, 0, cuts[0] : cuts[1]].reshape(rows, layers, 2, 2, half_head)
    query_bias = lax.dynamic_index_in_dim(query_bias, at_core, 3, keepdims=False)
    hidden_bias = small[:, 0, cuts[1] : cuts[2]].reshape(rows, layers, 2, half_hidden)
    hidden_bias = lax.dynamic_index_in_dim(hidden_bias, at_core, 2, keepdims=False)

    def to_chip(value):
        kept = lax.dynamic_slice_in_dim(value, at_pair * length, length, 1)
        given = lax.dynamic_slice_in_dim(value, (1 - at_pair) * length, length, 1)
        mine = jnp.stack([kept, swap(given, "pair")])
        whole = by_core(mine[:, None], swap(mine, "core")[:, None], 1)
        return whole.reshape(width, length).astype(jnp.float32).T

    residual = to_chip(tokens)
    gradient = to_chip(cotangent)

    stored = []
    for layer_at in range(layers):
        gain_one, shift_one, bias_out, gain_two, shift_two, bias_down = vectors[:, layer_at]
        mixing = attention_weights[layer_at]
        normed_one, unit_one, inverse_one = norm_forward(residual, gain_one, shift_one)
        mixed = []
        for row in range(rows):
            offsets = jnp.concatenate(
                [
                    query_bias[row, layer_at, 0],
                    jnp.zeros((half_head,), jnp.float32),
                    query_bias[row, layer_at, 1],
                ]
            )
            produced = plain(normed_one, mixing[row][:, : 3 * half_head]) + offsets
            mixed.append(produced.astype(jnp.bfloat16).reshape(length, 3, half_head))
        mixed = jnp.concatenate(mixed, axis=2)
        heads = [by_heads(mixed[:, part]) for part in range(3)]
        attended, logsum = attend_forward(*heads, document)
        attended_low = from_heads(attended.astype(jnp.bfloat16))
        branch = sum(
            contract_cols(
                attended_low[:, row * half_head : (row + 1) * half_head],
                mixing[row][:, 3 * half_head :],
            )
            for row in range(rows)
        )
        middle = residual + (pair_sum(branch) + bias_out)
        normed_two, unit_two, inverse_two = norm_forward(middle, gain_two, shift_two)
        wide = forward_weights[layer_at]
        upward = [
            plain(normed_two, wide[row][:, :half_hidden]) + hidden_bias[row, layer_at]
            for row in range(rows)
        ]
        active = [jax.nn.gelu(part, approximate=True).astype(jnp.bfloat16) for part in upward]
        branch_two = sum(
            contract_cols(active[row], wide[row][:, half_hidden:]) for row in range(rows)
        )
        stored.append(
            (
                normed_one,
                unit_one,
                inverse_one,
                heads,
                logsum,
                attended_low,
                normed_two,
                unit_two,
                inverse_two,
                upward,
                active,
            )
        )
        residual = middle + (pair_sum(branch_two) + bias_down)

    def to_owner(value):
        blocks = value.T.reshape(pairs, 2, depth_in, length)
        blocks = jnp.where(at_core == 0, blocks[:, 0], blocks[:, 1])
        kept, came = blocks[0], swap(blocks[1], "pair")
        first = at_pair == 0
        return jnp.concatenate(
            [jnp.where(first, kept, came), jnp.where(first, came, kept)], axis=1
        )

    activations = to_owner(residual.astype(jnp.bfloat16))

    vector_parts = [None] * layers
    attention_grads = [None] * layers
    forward_grads = [None] * layers
    for layer_at in reversed(range(layers)):
        (
            normed_one,
            unit_one,
            inverse_one,
            heads,
            logsum,
            attended_low,
            normed_two,
            unit_two,
            inverse_two,
            upward,
            active,
        ) = stored[layer_at]
        gain_one, _, _, gain_two, _, _ = vectors[:, layer_at]
        mixing, wide = attention_weights[layer_at], forward_weights[layer_at]
        down_in = gradient.astype(jnp.bfloat16)
        hidden_grads = []
        parts = []
        normed_grad = 0.0
        for row in range(rows):
            down_grad = contract_rows(down_in, active[row])
            active_grad = plain(down_in, wide[row][:, half_hidden:])
            _, gelu_pull = jax.vjp(partial(jax.nn.gelu, approximate=True), upward[row])
            hidden_grad = gelu_pull(active_grad)[0].astype(jnp.bfloat16)
            up_grad = contract_rows(normed_two, hidden_grad)
            normed_grad = normed_grad + contract_cols(hidden_grad, wide[row][:, :half_hidden])
            hidden_grads.append(jnp.sum(hidden_grad.astype(jnp.float32), axis=0))
            parts.append(jnp.concatenate([up_grad, down_grad], axis=1))
        summed = scatter_plane(parts)
        if layer_at + 1 < layers:
            summed = chained(summed, attention_grads[layer_at + 1])
        forward_grads[layer_at] = lax.psum(summed, "dp")
        back_two, gain_two_grad, shift_two_grad = norm_backward(
            pair_sum(normed_grad), unit_two, inverse_two, gain_two
        )
        middle_grad = gradient + back_two
        out_in = middle_grad.astype(jnp.bfloat16)
        out_grads = []
        attended_grad = []
        for row in range(rows):
            span = slice(row * half_head, (row + 1) * half_head)
            out_grads.append(contract_rows(out_in, attended_low[:, span]))
            attended_grad.append(plain(out_in, mixing[row][:, 3 * half_head :]))
        attended_grad = jnp.concatenate(attended_grad, axis=1).astype(jnp.bfloat16)
        mixed_grad = [
            from_heads(part.astype(jnp.bfloat16))
            for part in attend_backward(*heads, document, logsum, by_heads(attended_grad))
        ]
        parts = []
        normed_grad = 0.0
        for row in range(rows):
            span = slice(row * half_head, (row + 1) * half_head)
            pieces = jnp.concatenate([part[:, span] for part in mixed_grad], axis=1)
            parts.append(
                jnp.concatenate([contract_rows(normed_one, pieces), out_grads[row]], axis=1)
            )
            normed_grad = normed_grad + contract_cols(pieces, mixing[row][:, : 3 * half_head])
        summed = chained(scatter_plane(parts), forward_grads[layer_at])
        attention_grads[layer_at] = lax.psum(summed, "dp")
        back_one, gain_one_grad, shift_one_grad = norm_backward(
            pair_sum(normed_grad), unit_one, inverse_one, gain_one
        )
        query_sums = jnp.stack(
            [jnp.sum(mixed_grad[part].astype(jnp.float32), axis=0) for part in (0, 2)]
        )
        vector_parts[layer_at] = (
            jnp.stack(
                [
                    gain_one_grad,
                    shift_one_grad,
                    jnp.sum(out_in.astype(jnp.float32), axis=0),
                    gain_two_grad,
                    shift_two_grad,
                    jnp.sum(down_in.astype(jnp.float32), axis=0),
                ]
            ),
            query_sums.reshape(2, rows, half_head),
            jnp.stack(hidden_grads),
        )
        gradient = middle_grad + back_one

    input_grad = to_owner(gradient)
    deep, asked, hidden = (
        jnp.stack([vector_parts[layer_at][part] for layer_at in range(layers)]) for part in range(3)
    )
    deep = deep.reshape(layers, 6, pairs, 2 * depth_in)
    deep = jnp.where(at_pair == 0, deep, deep[:, :, ::-1])
    asked = jnp.where(at_row == 0, asked, asked[:, :, ::-1])
    hidden = jnp.where(at_row == 0, hidden, hidden[:, ::-1])
    sums = lax.psum(
        jnp.concatenate([deep.reshape(-1), asked.reshape(-1), hidden.reshape(-1)]),
        ("dp", "row", "pair"),
    )
    hidden_sums = by_core(
        sums[None, deep.size :], swap(sums[deep.size :], "core")[None], 0
    )
    deep_sums = lax.dynamic_slice_in_dim(
        sums[: deep.size].reshape(layers, 6, width), (at_pair * 2 + at_core) * depth_in, depth_in, 2
    )
    asked_sums = hidden_sums[:, : asked.size].reshape(2, layers, 2, rows, half_head)
    asked_sums = lax.dynamic_index_in_dim(asked_sums, at_row, 3, keepdims=False)
    asked_sums = asked_sums.transpose(1, 2, 0, 3).reshape(layers, 2, head_width)
    up_sums = hidden_sums[:, asked.size :].reshape(2, layers, rows, half_hidden)
    up_sums = lax.dynamic_index_in_dim(up_sums, at_row, 2, keepdims=False)
    up_sums = up_sums.transpose(1, 0, 2).reshape(layers, hidden_width)

    attention_out = jnp.stack([return_weights(part) for part in attention_grads])
    forward_out = jnp.stack([return_weights(part) for part in forward_grads])
    qkv_grad = attention_out[..., : 3 * half_head].reshape(layers, depth_in, 2, 3, half_head)
    qkv_grad = qkv_grad.transpose(0, 1, 3, 2, 4).reshape(layers, depth_in, 3, head_width)
    out_grad = attention_out[..., 3 * half_head :].reshape(layers, depth_in, head_width)
    up_grad = forward_out[..., :half_hidden].reshape(layers, depth_in, hidden_width)
    down_grad = forward_out[..., half_hidden:].reshape(layers, depth_in, hidden_width)
    return (
        activations,
        input_grad,
        deep_sums[:, 0],
        deep_sums[:, 1],
        qkv_grad,
        asked_sums,
        out_grad,
        deep_sums[:, 2],
        deep_sums[:, 3],
        deep_sums[:, 4],
        up_grad,
        up_sums,
        down_grad,
        deep_sums[:, 5],
    )


def solution(mesh):
    devices = mesh.devices
    depth, rows, cols = devices.shape
    chips = Mesh(devices.reshape(depth, rows, cols // 2, 2), ("dp", "row", "pair", "core"))
    col = ("pair", "core")
    placed = (
        P(col, ("dp", "row")),
        P(col, ("dp", "row")),
        P(("dp", "pair", "core"), None),
        P(None, col),
        P(None, col),
        P(None, col, None, "row"),
        P(None, None, "row"),
        P(None, col, "row"),
        P(None, col),
        P(None, col),
        P(None, col),
        P(None, col, "row"),
        P(None, "row"),
        P(None, col, "row"),
        P(None, col),
    )
    return jax.shard_map(
        shards,
        mesh=chips,
        in_specs=placed,
        out_specs=(
            P(col, ("dp", "row")),
            P(col, ("dp", "row")),
            P(None, col),
            P(None, col),
            P(None, col, None, "row"),
            P(None, None, "row"),
            P(None, col, "row"),
            P(None, col),
            P(None, col),
            P(None, col),
            P(None, col, "row"),
            P(None, "row"),
            P(None, col, "row"),
            P(None, col),
        ),
        check_vma=False,
    )
```

```python
from functools import partial

import jax
import jax.numpy as jnp
from jax import lax
from jax.sharding import Mesh, PartitionSpec as P

HEAD_DIM = 64
EPSILON = 1e-05
NEGATIVE = -1e30
PLANE = ("row", "pair")


def contract_rows(left_side, right_side):
    return lax.dot_general(
        left_side, right_side, (((0,), (0,)), ((), ())), preferred_element_type=jnp.float32
    )


def contract_cols(left_side, right_side):
    return lax.dot_general(
        left_side, right_side, (((1,), (1,)), ((), ())), preferred_element_type=jnp.float32
    )


def plain(left_side, right_side):
    return jnp.dot(left_side, right_side, preferred_element_type=jnp.float32)


def pair_sum(value):
    return value + lax.ppermute(value, "core", [(0, 1), (1, 0)])


def norm_forward(residual, gain_vec, shift_vec):
    average = jnp.mean(residual, axis=1, keepdims=True)
    variance = jnp.mean(residual * residual, axis=1, keepdims=True) - average * average
    inverse = lax.rsqrt(variance + EPSILON)
    unit_rows = (residual - average) * inverse
    return ((unit_rows * gain_vec + shift_vec).astype(jnp.bfloat16), unit_rows, inverse)


def norm_backward(upstream, unit_rows, inverse, gain_vec):
    scaled = upstream * gain_vec
    first = jnp.mean(scaled, axis=1, keepdims=True)
    second = jnp.mean(scaled * unit_rows, axis=1, keepdims=True)
    result = inverse * (scaled - first - unit_rows * second)
    return (result, jnp.sum(upstream * unit_rows, axis=0), jnp.sum(upstream, axis=0))


def masked_scores(queries, keys_block, document):
    length = document.shape[0]
    position = jnp.arange(length)
    allowed = (position[:, None] >= position[None, :]) & (document[:, None] == document[None, :])
    scores = jnp.einsum(
        "hqd,hkd->hqk", queries, keys_block, preferred_element_type=jnp.float32
    ) * HEAD_DIM ** (-0.5)
    return jnp.where(allowed[None], scores, NEGATIVE)


def by_heads(value):
    return value.reshape(value.shape[0], -1, HEAD_DIM).transpose(1, 0, 2)


def from_heads(value):
    return value.transpose(1, 0, 2).reshape(value.shape[1], -1)


def attend_forward(queries, keys_block, values_block, document):
    scores = masked_scores(queries, keys_block, document)
    highest = jnp.max(scores, axis=-1, keepdims=True)
    exponent = jnp.exp(scores - highest)
    denominator = jnp.sum(exponent, axis=-1, keepdims=True)
    weights_low = (exponent / denominator).astype(jnp.bfloat16)
    attended = jnp.einsum(
        "hqk,hkd->hqd", weights_low, values_block, preferred_element_type=jnp.float32
    )
    return (attended, highest + jnp.log(denominator))


def attend_backward(queries, keys_block, values_block, document, logsum, out_grad):
    factor = HEAD_DIM ** (-0.5)
    probs = jnp.exp(masked_scores(queries, keys_block, document) - logsum)
    value_grad = jnp.einsum(
        "hqk,hqd->hkd", probs.astype(jnp.bfloat16), out_grad, preferred_element_type=jnp.float32
    )
    prob_grad = jnp.einsum(
        "hqd,hkd->hqk", out_grad, values_block, preferred_element_type=jnp.float32
    )
    inner_sum = jnp.sum(probs * prob_grad, axis=-1, keepdims=True)
    score_grad = (probs * (prob_grad - inner_sum)).astype(jnp.bfloat16)
    query_grad = (
        jnp.einsum("hqk,hkd->hqd", score_grad, keys_block, preferred_element_type=jnp.float32)
        * factor
    )
    key_grad = (
        jnp.einsum("hqk,hqd->hkd", score_grad, queries, preferred_element_type=jnp.float32)
        * factor
    )
    return query_grad, key_grad, value_grad


def swap(value, axis):
    return lax.ppermute(value, axis, [(0, 1), (1, 0)])


def in_order(name, mine, other, axis):
    first = lax.axis_index(name) == 0
    return jnp.concatenate([jnp.where(first, mine, other), jnp.where(first, other, mine)], axis)


def share_weights(parts):
    joined = jnp.concatenate(parts, axis=-1)
    first = lax.axis_index("core") == 0
    kept = jnp.where(first, joined[:, 0], joined[:, 1])
    given = jnp.where(first, joined[:, 1], joined[:, 0])
    return in_order("core", kept, swap(given, "core"), 0)


def gather_plane(piece):
    everything = lax.all_gather(piece, PLANE, axis=0, tiled=False)
    rows = lax.axis_size("row")
    return everything.reshape(rows, -1, piece.shape[-1])


def scatter_plane(grads):
    pairs = lax.axis_size("pair")
    stacked = jnp.stack(grads).astype(jnp.bfloat16)
    stacked = stacked.reshape(len(grads) * pairs, -1, stacked.shape[-1])
    return lax.optimization_barrier(
        lax.psum_scatter(stacked, PLANE, scatter_dimension=0, tiled=False)
    )


def partners(step):
    size = lax.axis_size("dp")
    return [(place, place ^ step) for place in range(size)]


def group_sum(value):
    size, place = lax.axis_size("dp"), lax.axis_index("dp")
    if size & (size - 1):
        return lax.psum(value, "dp")
    step = 1
    while step < size:
        half = value.shape[0] // 2
        upper = (place // step) % 2 == 1
        kept = jnp.where(upper, value[half:], value[:half])
        given = jnp.where(upper, value[:half], value[half:])
        came = lax.ppermute(given, "dp", partners(step))
        value = (kept.astype(jnp.float32) + came.astype(jnp.float32)).astype(jnp.bfloat16)
        step *= 2
    while step > 1:
        step //= 2
        upper = (place // step) % 2 == 1
        came = lax.ppermute(value, "dp", partners(step))
        value = jnp.concatenate([jnp.where(upper, came, value), jnp.where(upper, value, came)])
    return value


def vector_sum(value):
    value = value + swap(value, "row")
    value = value + swap(value, "pair")
    size = lax.axis_size("dp")
    if size & (size - 1):
        return lax.psum(value, "dp")
    step = 1
    while step < size:
        value = value + lax.ppermute(value, "dp", partners(step))
        step *= 2
    return value


def return_weights(piece):
    piece = piece.reshape(2, -1, piece.shape[-1])
    first = lax.axis_index("core") == 0
    kept = jnp.where(first, piece[0], piece[1])
    given = jnp.where(first, piece[1], piece[0])
    return in_order("core", kept[:, None], swap(given, "core")[:, None], 1).astype(jnp.float32)


def shards(
    tokens,
    cotangent,
    segments,
    first_gain,
    first_shift,
    qkv_weight,
    qv_bias,
    out_weight,
    out_bias,
    second_gain,
    second_shift,
    up_weight,
    up_bias,
    down_weight,
    down_bias,
):
    layers, depth_in, _, head_width = qkv_weight.shape
    hidden_width = up_weight.shape[2]
    half_head, half_hidden = head_width // 2, hidden_width // 2
    rows, pairs = lax.axis_size("row"), lax.axis_size("pair")
    at_row, at_pair, at_core = (lax.axis_index(name) for name in ("row", "pair", "core"))
    width = depth_in * pairs * 2
    length = segments.shape[1]

    attention_weights = []
    forward_weights = []
    for layer_at in range(layers):
        gathered = gather_plane(
            share_weights(
                [
                    up_weight[layer_at].reshape(depth_in, 2, half_hidden),
                    down_weight[layer_at].reshape(depth_in, 2, half_hidden),
                    qkv_weight[layer_at]
                    .reshape(depth_in, 3, 2, half_head)
                    .transpose(0, 2, 1, 3)
                    .reshape(depth_in, 2, 3 * half_head),
                    out_weight[layer_at].reshape(depth_in, 2, half_head),
                ]
            )
        )
        forward_weights.append(gathered[..., : 2 * half_hidden])
        attention_weights.append(gathered[..., 2 * half_hidden :])

    small = jnp.concatenate(
        [
            jnp.stack(
                [first_gain, first_shift, out_bias, second_gain, second_shift, down_bias]
            ).reshape(-1),
            qv_bias.reshape(-1),
            up_bias.reshape(-1),
            segments[0].astype(jnp.bfloat16),
        ]
    )
    small = lax.all_gather(small, ("row", "pair", "core"), axis=0, tiled=False).astype(jnp.float32)
    small = small.reshape(rows, pairs * 2, -1)
    cuts = [6 * layers * depth_in, 2 * layers * head_width, layers * hidden_width]
    cuts = [cuts[0], cuts[0] + cuts[1], cuts[0] + cuts[1] + cuts[2]]
    vectors = small[0, :, : cuts[0]].reshape(pairs * 2, 6, layers, depth_in)
    vectors = vectors.transpose(1, 2, 0, 3).reshape(6, layers, width)
    query_bias = small[:, 0, cuts[0] : cuts[1]].reshape(rows, layers, 2, 2, half_head)
    query_bias = lax.dynamic_index_in_dim(query_bias, at_core, 3, keepdims=False)
    hidden_bias = small[:, 0, cuts[1] : cuts[2]].reshape(rows, layers, 2, half_hidden)
    hidden_bias = lax.dynamic_index_in_dim(hidden_bias, at_core, 2, keepdims=False)
    document = lax.dynamic_index_in_dim(
        small[0, :, cuts[2] :], at_row * pairs + at_pair, 0, keepdims=False
    )

    def to_chip(value):
        kept = lax.dynamic_slice_in_dim(value, at_pair * length, length, 1)
        given = lax.dynamic_slice_in_dim(value, (1 - at_pair) * length, length, 1)
        mine = in_order("pair", kept[None], swap(given, "pair")[None], 0)
        whole = in_order("core", mine[:, None], swap(mine, "core")[:, None], 1)
        return whole.reshape(width, length).astype(jnp.float32).T

    residual = to_chip(tokens)
    gradient = to_chip(cotangent)

    stored = []
    for layer_at in range(layers):
        gain_one, shift_one, bias_out, gain_two, shift_two, bias_down = vectors[:, layer_at]
        mixing = attention_weights[layer_at]
        normed_one, unit_one, inverse_one = norm_forward(residual, gain_one, shift_one)
        mixed = []
        for row in range(rows):
            offsets = jnp.concatenate(
                [
                    query_bias[row, layer_at, 0],
                    jnp.zeros((half_head,), jnp.float32),
                    query_bias[row, layer_at, 1],
                ]
            )
            produced = plain(normed_one, mixing[row][:, : 3 * half_head]) + offsets
            mixed.append(produced.astype(jnp.bfloat16).reshape(length, 3, half_head))
        mixed = jnp.concatenate(mixed, axis=2)
        heads = [by_heads(mixed[:, part]) for part in range(3)]
        attended, logsum = attend_forward(*heads, document)
        attended_low = from_heads(attended.astype(jnp.bfloat16))
        branch = sum(
            contract_cols(
                attended_low[:, row * half_head : (row + 1) * half_head],
                mixing[row][:, 3 * half_head :],
            )
            for row in range(rows)
        )
        middle = residual + (pair_sum(branch) + bias_out)
        normed_two, unit_two, inverse_two = norm_forward(middle, gain_two, shift_two)
        wide = forward_weights[layer_at]
        upward = [
            plain(normed_two, wide[row][:, :half_hidden]) + hidden_bias[row, layer_at]
            for row in range(rows)
        ]
        active = [jax.nn.gelu(part, approximate=True).astype(jnp.bfloat16) for part in upward]
        branch_two = sum(
            contract_cols(active[row], wide[row][:, half_hidden:]) for row in range(rows)
        )
        stored.append(
            (
                normed_one,
                unit_one,
                inverse_one,
                heads,
                logsum,
                attended_low,
                normed_two,
                unit_two,
                inverse_two,
                upward,
                active,
            )
        )
        residual = middle + (pair_sum(branch_two) + bias_down)

    def to_owner(value):
        blocks = value.T.reshape(pairs, 2, depth_in, length)
        blocks = jnp.where(at_core == 0, blocks[:, 0], blocks[:, 1])
        first = at_pair == 0
        kept = jnp.where(first, blocks[0], blocks[1])
        given = jnp.where(first, blocks[1], blocks[0])
        return in_order("pair", kept, swap(given, "pair"), 1)

    activations = to_owner(residual.astype(jnp.bfloat16))

    vector_parts = [None] * layers
    attention_grads = [None] * layers
    forward_grads = [None] * layers
    for layer_at in reversed(range(layers)):
        (
            normed_one,
            unit_one,
            inverse_one,
            heads,
            logsum,
            attended_low,
            normed_two,
            unit_two,
            inverse_two,
            upward,
            active,
        ) = stored[layer_at]
        gain_one, _, _, gain_two, _, _ = vectors[:, layer_at]
        mixing, wide = attention_weights[layer_at], forward_weights[layer_at]
        down_in = gradient.astype(jnp.bfloat16)
        hidden_grads = []
        parts = []
        normed_grad = 0.0
        for row in range(rows):
            down_grad = contract_rows(down_in, active[row])
            active_grad = plain(down_in, wide[row][:, half_hidden:])
            _, gelu_pull = jax.vjp(partial(jax.nn.gelu, approximate=True), upward[row])
            hidden_grad = gelu_pull(active_grad)[0].astype(jnp.bfloat16)
            up_grad = contract_rows(normed_two, hidden_grad)
            normed_grad = normed_grad + contract_cols(hidden_grad, wide[row][:, :half_hidden])
            hidden_grads.append(jnp.sum(hidden_grad.astype(jnp.float32), axis=0))
            parts.append(jnp.concatenate([up_grad, down_grad], axis=1))
        forward_grads[layer_at] = scatter_plane(parts)
        back_two, gain_two_grad, shift_two_grad = norm_backward(
            pair_sum(normed_grad), unit_two, inverse_two, gain_two
        )
        middle_grad = gradient + back_two
        out_in = middle_grad.astype(jnp.bfloat16)
        out_grads = []
        attended_grad = []
        for row in range(rows):
            span = slice(row * half_head, (row + 1) * half_head)
            out_grads.append(contract_rows(out_in, attended_low[:, span]))
            attended_grad.append(plain(out_in, mixing[row][:, 3 * half_head :]))
        attended_grad = jnp.concatenate(attended_grad, axis=1).astype(jnp.bfloat16)
        mixed_grad = [
            from_heads(part.astype(jnp.bfloat16))
            for part in attend_backward(*heads, document, logsum, by_heads(attended_grad))
        ]
        parts = []
        normed_grad = 0.0
        for row in range(rows):
            span = slice(row * half_head, (row + 1) * half_head)
            pieces = jnp.concatenate([part[:, span] for part in mixed_grad], axis=1)
            parts.append(
                jnp.concatenate([contract_rows(normed_one, pieces), out_grads[row]], axis=1)
            )
            normed_grad = normed_grad + contract_cols(pieces, mixing[row][:, : 3 * half_head])
        attention_grads[layer_at] = scatter_plane(parts)
        back_one, gain_one_grad, shift_one_grad = norm_backward(
            pair_sum(normed_grad), unit_one, inverse_one, gain_one
        )
        query_sums = jnp.stack(
            [jnp.sum(mixed_grad[part].astype(jnp.float32), axis=0) for part in (0, 2)]
        )
        vector_parts[layer_at] = (
            jnp.stack(
                [
                    gain_one_grad,
                    shift_one_grad,
                    jnp.sum(out_in.astype(jnp.float32), axis=0),
                    gain_two_grad,
                    shift_two_grad,
                    jnp.sum(down_in.astype(jnp.float32), axis=0),
                ]
            ),
            query_sums.reshape(2, rows, half_head),
            jnp.stack(hidden_grads),
        )
        gradient = middle_grad + back_one

    first_parts = [(attention_grads[layer], forward_grads[layer]) for layer in range(1, layers)]
    gradient, first_parts = lax.optimization_barrier((gradient, first_parts))
    for layer_at in range(1, layers):
        attention_grads[layer_at], forward_grads[layer_at] = first_parts[layer_at - 1]
    for layer_at in reversed(range(layers)):
        forward_grads[layer_at] = group_sum(forward_grads[layer_at])
        attention_grads[layer_at] = group_sum(attention_grads[layer_at])
    input_grad = to_owner(gradient)
    deep, asked, hidden = (
        jnp.stack([vector_parts[layer_at][part] for layer_at in range(layers)]) for part in range(3)
    )
    sums = vector_sum(
        jnp.concatenate([deep.reshape(-1), asked.reshape(-1), hidden.reshape(-1)])
    )
    ours = sums[deep.size :]
    hidden_sums = in_order("core", ours[None], swap(ours, "core")[None], 0)
    deep_sums = lax.dynamic_slice_in_dim(
        sums[: deep.size].reshape(layers, 6, width), (at_pair * 2 + at_core) * depth_in, depth_in, 2
    )
    asked_sums = hidden_sums[:, : asked.size].reshape(2, layers, 2, rows, half_head)
    asked_sums = lax.dynamic_index_in_dim(asked_sums, at_row, 3, keepdims=False)
    asked_sums = asked_sums.transpose(1, 2, 0, 3).reshape(layers, 2, head_width)
    up_sums = hidden_sums[:, asked.size :].reshape(2, layers, rows, half_hidden)
    up_sums = lax.dynamic_index_in_dim(up_sums, at_row, 2, keepdims=False)
    up_sums = up_sums.transpose(1, 0, 2).reshape(layers, hidden_width)

    attention_out = jnp.stack([return_weights(part) for part in attention_grads])
    forward_out = jnp.stack([return_weights(part) for part in forward_grads])
    qkv_grad = attention_out[..., : 3 * half_head].reshape(layers, depth_in, 2, 3, half_head)
    qkv_grad = qkv_grad.transpose(0, 1, 3, 2, 4).reshape(layers, depth_in, 3, head_width)
    out_grad = attention_out[..., 3 * half_head :].reshape(layers, depth_in, head_width)
    up_grad = forward_out[..., :half_hidden].reshape(layers, depth_in, hidden_width)
    down_grad = forward_out[..., half_hidden:].reshape(layers, depth_in, hidden_width)
    return (
        activations,
        input_grad,
        deep_sums[:, 0],
        deep_sums[:, 1],
        qkv_grad,
        asked_sums,
        out_grad,
        deep_sums[:, 2],
        deep_sums[:, 3],
        deep_sums[:, 4],
        up_grad,
        up_sums,
        down_grad,
        deep_sums[:, 5],
    )


def solution(mesh):
    devices = mesh.devices
    depth, rows, cols = devices.shape
    chips = Mesh(devices.reshape(depth, rows, cols // 2, 2), ("dp", "row", "pair", "core"))
    col = ("pair", "core")
    placed = (
        P(col, ("dp", "row")),
        P(col, ("dp", "row")),
        P(("dp", "pair", "core"), None),
        P(None, col),
        P(None, col),
        P(None, col, None, "row"),
        P(None, None, "row"),
        P(None, col, "row"),
        P(None, col),
        P(None, col),
        P(None, col),
        P(None, col, "row"),
        P(None, "row"),
        P(None, col, "row"),
        P(None, col),
    )
    return jax.shard_map(
        shards,
        mesh=chips,
        in_specs=placed,
        out_specs=(
            P(col, ("dp", "row")),
            P(col, ("dp", "row")),
            P(None, col),
            P(None, col),
            P(None, col, None, "row"),
            P(None, None, "row"),
            P(None, col, "row"),
            P(None, col),
            P(None, col),
            P(None, col),
            P(None, col, "row"),
            P(None, "row"),
            P(None, col, "row"),
            P(None, col),
        ),
        check_vma=False,
    )
```

```python
from functools import partial

import jax
import jax.numpy as jnp
from jax import lax
from jax.sharding import Mesh, PartitionSpec as P

HEAD_DIM = 64
EPSILON = 1e-05
NEGATIVE = -1e30
PLANE = ("row", "pair")


def contract_rows(left_side, right_side):
    return lax.dot_general(
        left_side, right_side, (((0,), (0,)), ((), ())), preferred_element_type=jnp.float32
    )


def contract_cols(left_side, right_side):
    return lax.dot_general(
        left_side, right_side, (((1,), (1,)), ((), ())), preferred_element_type=jnp.float32
    )


def plain(left_side, right_side):
    return jnp.dot(left_side, right_side, preferred_element_type=jnp.float32)


def pair_sum(value):
    return value + lax.ppermute(value, "core", [(0, 1), (1, 0)])


def norm_forward(residual, gain_vec, shift_vec):
    average = jnp.mean(residual, axis=1, keepdims=True)
    variance = jnp.mean(residual * residual, axis=1, keepdims=True) - average * average
    inverse = lax.rsqrt(variance + EPSILON)
    unit_rows = (residual - average) * inverse
    return ((unit_rows * gain_vec + shift_vec).astype(jnp.bfloat16), unit_rows, inverse)


def norm_backward(upstream, unit_rows, inverse, gain_vec):
    scaled = upstream * gain_vec
    first = jnp.mean(scaled, axis=1, keepdims=True)
    second = jnp.mean(scaled * unit_rows, axis=1, keepdims=True)
    result = inverse * (scaled - first - unit_rows * second)
    return (result, jnp.sum(upstream * unit_rows, axis=0), jnp.sum(upstream, axis=0))


def masked_scores(queries, keys_block, document):
    length = document.shape[0]
    position = jnp.arange(length)
    allowed = (position[:, None] >= position[None, :]) & (document[:, None] == document[None, :])
    scores = jnp.einsum(
        "hqd,hkd->hqk", queries, keys_block, preferred_element_type=jnp.float32
    ) * HEAD_DIM ** (-0.5)
    return jnp.where(allowed[None], scores, NEGATIVE)


def by_heads(value):
    return value.reshape(value.shape[0], -1, HEAD_DIM).transpose(1, 0, 2)


def from_heads(value):
    return value.transpose(1, 0, 2).reshape(value.shape[1], -1)


def attend_forward(queries, keys_block, values_block, document):
    scores = masked_scores(queries, keys_block, document)
    highest = jnp.max(scores, axis=-1, keepdims=True)
    exponent = jnp.exp(scores - highest)
    denominator = jnp.sum(exponent, axis=-1, keepdims=True)
    weights_low = (exponent / denominator).astype(jnp.bfloat16)
    attended = jnp.einsum(
        "hqk,hkd->hqd", weights_low, values_block, preferred_element_type=jnp.float32
    )
    return (attended, highest + jnp.log(denominator))


def attend_backward(queries, keys_block, values_block, document, logsum, out_grad):
    factor = HEAD_DIM ** (-0.5)
    probs = jnp.exp(masked_scores(queries, keys_block, document) - logsum)
    value_grad = jnp.einsum(
        "hqk,hqd->hkd", probs.astype(jnp.bfloat16), out_grad, preferred_element_type=jnp.float32
    )
    prob_grad = jnp.einsum(
        "hqd,hkd->hqk", out_grad, values_block, preferred_element_type=jnp.float32
    )
    inner_sum = jnp.sum(probs * prob_grad, axis=-1, keepdims=True)
    score_grad = (probs * (prob_grad - inner_sum)).astype(jnp.bfloat16)
    query_grad = (
        jnp.einsum("hqk,hkd->hqd", score_grad, keys_block, preferred_element_type=jnp.float32)
        * factor
    )
    key_grad = (
        jnp.einsum("hqk,hqd->hkd", score_grad, queries, preferred_element_type=jnp.float32)
        * factor
    )
    return query_grad, key_grad, value_grad


def swap(value, axis):
    return lax.ppermute(value, axis, [(0, 1), (1, 0)])


def in_order(name, mine, other, axis):
    first = lax.axis_index(name) == 0
    return jnp.concatenate([jnp.where(first, mine, other), jnp.where(first, other, mine)], axis)


def share_weights(parts):
    first = lax.axis_index("core") == 0
    kept, given = [], []
    for part in parts:
        half = part.shape[-1] // 2
        lower, upper = part[..., :half], part[..., half:]
        kept.append(jnp.where(first, lower, upper).reshape(part.shape[0], -1))
        given.append(jnp.where(first, upper, lower).reshape(part.shape[0], -1))
    kept, given = jnp.concatenate(kept, axis=1), jnp.concatenate(given, axis=1)
    return in_order("core", kept, swap(given, "core"), 0)


def gather_plane(piece):
    everything = lax.all_gather(piece, PLANE, axis=0, tiled=False)
    rows = lax.axis_size("row")
    return everything.reshape(rows, -1, piece.shape[-1])


def scatter_plane(grads):
    pairs = lax.axis_size("pair")
    stacked = jnp.stack(grads).astype(jnp.bfloat16)
    stacked = stacked.reshape(len(grads) * pairs, -1, stacked.shape[-1])
    return lax.optimization_barrier(
        lax.psum_scatter(stacked, PLANE, scatter_dimension=0, tiled=False)
    )


def partners(step):
    size = lax.axis_size("dp")
    return [(place, place ^ step) for place in range(size)]


def group_sum(value):
    size, place = lax.axis_size("dp"), lax.axis_index("dp")
    if size & (size - 1):
        return lax.psum(value, "dp")
    step = 1
    while step < size:
        half = value.shape[0] // 2
        upper = (place // step) % 2 == 1
        kept = jnp.where(upper, value[half:], value[:half])
        given = jnp.where(upper, value[:half], value[half:])
        came = lax.ppermute(given, "dp", partners(step))
        value = (kept.astype(jnp.float32) + came.astype(jnp.float32)).astype(jnp.bfloat16)
        step *= 2
    while step > 1:
        step //= 2
        upper = (place // step) % 2 == 1
        came = lax.ppermute(value, "dp", partners(step))
        value = jnp.concatenate([jnp.where(upper, came, value), jnp.where(upper, value, came)])
    return value


def vector_sum(value):
    value = value + swap(value, "row")
    value = value + swap(value, "pair")
    size = lax.axis_size("dp")
    if size & (size - 1):
        return lax.psum(value, "dp")
    step = 1
    while step < size:
        value = value + lax.ppermute(value, "dp", partners(step))
        step *= 2
    return value


def return_weights(piece):
    piece = piece.reshape(2, -1, piece.shape[-1])
    first = lax.axis_index("core") == 0
    kept = jnp.where(first, piece[0], piece[1])
    came = swap(jnp.where(first, piece[1], piece[0]), "core")
    return jnp.where(first, kept, came), jnp.where(first, came, kept)


def join_halves(pieces, start, stop, inner):
    shaped = [part[:, start:stop].reshape((-1,) + inner) for part in pieces]
    return jnp.concatenate(shaped, axis=-1).astype(jnp.float32)


def shards(
    tokens,
    cotangent,
    segments,
    first_gain,
    first_shift,
    qkv_weight,
    qv_bias,
    out_weight,
    out_bias,
    second_gain,
    second_shift,
    up_weight,
    up_bias,
    down_weight,
    down_bias,
):
    layers, depth_in, _, head_width = qkv_weight.shape
    hidden_width = up_weight.shape[2]
    half_head, half_hidden = head_width // 2, hidden_width // 2
    rows, pairs = lax.axis_size("row"), lax.axis_size("pair")
    at_row, at_pair, at_core = (lax.axis_index(name) for name in ("row", "pair", "core"))
    width = depth_in * pairs * 2
    length = segments.shape[1]

    attention_weights = []
    forward_weights = []
    for layer_at in range(layers):
        gathered = gather_plane(
            share_weights(
                [
                    up_weight[layer_at],
                    down_weight[layer_at],
                    qkv_weight[layer_at],
                    out_weight[layer_at],
                ]
            )
        )
        forward_weights.append(gathered[..., : 2 * half_hidden])
        attention_weights.append(gathered[..., 2 * half_hidden :])

    small = jnp.concatenate(
        [
            jnp.stack(
                [first_gain, first_shift, out_bias, second_gain, second_shift, down_bias]
            ).reshape(-1),
            qv_bias.reshape(-1),
            up_bias.reshape(-1),
            segments[0].astype(jnp.bfloat16),
        ]
    )
    small = lax.all_gather(small, ("row", "pair", "core"), axis=0, tiled=False).astype(jnp.float32)
    small = small.reshape(rows, pairs * 2, -1)
    cuts = [6 * layers * depth_in, 2 * layers * head_width, layers * hidden_width]
    cuts = [cuts[0], cuts[0] + cuts[1], cuts[0] + cuts[1] + cuts[2]]
    vectors = small[0, :, : cuts[0]].reshape(pairs * 2, 6, layers, depth_in)
    vectors = vectors.transpose(1, 2, 0, 3).reshape(6, layers, width)
    query_bias = small[:, 0, cuts[0] : cuts[1]].reshape(rows, layers, 2, 2, half_head)
    query_bias = lax.dynamic_index_in_dim(query_bias, at_core, 3, keepdims=False)
    hidden_bias = small[:, 0, cuts[1] : cuts[2]].reshape(rows, layers, 2, half_hidden)
    hidden_bias = lax.dynamic_index_in_dim(hidden_bias, at_core, 2, keepdims=False)
    document = lax.dynamic_index_in_dim(
        small[0, :, cuts[2] :], at_row * pairs + at_pair, 0, keepdims=False
    )

    def to_chip(value):
        kept = lax.dynamic_slice_in_dim(value, at_pair * length, length, 1)
        given = lax.dynamic_slice_in_dim(value, (1 - at_pair) * length, length, 1)
        mine = in_order("pair", kept[None], swap(given, "pair")[None], 0)
        whole = in_order("core", mine[:, None], swap(mine, "core")[:, None], 1)
        return whole.reshape(width, length).astype(jnp.float32).T

    residual = to_chip(tokens)
    gradient = to_chip(cotangent)

    stored = []
    for layer_at in range(layers):
        gain_one, shift_one, bias_out, gain_two, shift_two, bias_down = vectors[:, layer_at]
        mixing = attention_weights[layer_at]
        normed_one, unit_one, inverse_one = norm_forward(residual, gain_one, shift_one)
        mixed = []
        for row in range(rows):
            offsets = jnp.concatenate(
                [
                    query_bias[row, layer_at, 0],
                    jnp.zeros((half_head,), jnp.float32),
                    query_bias[row, layer_at, 1],
                ]
            )
            produced = plain(normed_one, mixing[row][:, : 3 * half_head]) + offsets
            mixed.append(produced.astype(jnp.bfloat16).reshape(length, 3, half_head))
        mixed = jnp.concatenate(mixed, axis=2)
        heads = [by_heads(mixed[:, part]) for part in range(3)]
        attended, logsum = attend_forward(*heads, document)
        attended_low = from_heads(attended.astype(jnp.bfloat16))
        branch = sum(
            contract_cols(
                attended_low[:, row * half_head : (row + 1) * half_head],
                mixing[row][:, 3 * half_head :],
            )
            for row in range(rows)
        )
        middle = residual + (pair_sum(branch) + bias_out)
        normed_two, unit_two, inverse_two = norm_forward(middle, gain_two, shift_two)
        wide = forward_weights[layer_at]
        upward = [
            plain(normed_two, wide[row][:, :half_hidden]) + hidden_bias[row, layer_at]
            for row in range(rows)
        ]
        active = [jax.nn.gelu(part, approximate=True).astype(jnp.bfloat16) for part in upward]
        branch_two = sum(
            contract_cols(active[row], wide[row][:, half_hidden:]) for row in range(rows)
        )
        stored.append(
            (
                normed_one,
                unit_one,
                inverse_one,
                heads,
                logsum,
                attended_low,
                normed_two,
                unit_two,
                inverse_two,
                upward,
                active,
            )
        )
        residual = middle + (pair_sum(branch_two) + bias_down)

    def to_owner(value):
        blocks = value.T.reshape(pairs, 2, depth_in, length)
        blocks = jnp.where(at_core == 0, blocks[:, 0], blocks[:, 1])
        first = at_pair == 0
        kept = jnp.where(first, blocks[0], blocks[1])
        given = jnp.where(first, blocks[1], blocks[0])
        return in_order("pair", kept, swap(given, "pair"), 1)

    activations = to_owner(residual.astype(jnp.bfloat16))

    vector_parts = [None] * layers
    attention_grads = [None] * layers
    forward_grads = [None] * layers
    for layer_at in reversed(range(layers)):
        (
            normed_one,
            unit_one,
            inverse_one,
            heads,
            logsum,
            attended_low,
            normed_two,
            unit_two,
            inverse_two,
            upward,
            active,
        ) = stored[layer_at]
        gain_one, _, _, gain_two, _, _ = vectors[:, layer_at]
        mixing, wide = attention_weights[layer_at], forward_weights[layer_at]
        down_in = gradient.astype(jnp.bfloat16)
        hidden_grads = []
        parts = []
        normed_grad = 0.0
        for row in range(rows):
            down_grad = contract_rows(down_in, active[row])
            active_grad = plain(down_in, wide[row][:, half_hidden:])
            _, gelu_pull = jax.vjp(partial(jax.nn.gelu, approximate=True), upward[row])
            hidden_grad = gelu_pull(active_grad)[0].astype(jnp.bfloat16)
            up_grad = contract_rows(normed_two, hidden_grad)
            normed_grad = normed_grad + contract_cols(hidden_grad, wide[row][:, :half_hidden])
            hidden_grads.append(jnp.sum(hidden_grad.astype(jnp.float32), axis=0))
            parts.append(jnp.concatenate([up_grad, down_grad], axis=1))
        forward_grads[layer_at] = scatter_plane(parts)
        back_two, gain_two_grad, shift_two_grad = norm_backward(
            pair_sum(normed_grad), unit_two, inverse_two, gain_two
        )
        middle_grad = gradient + back_two
        out_in = middle_grad.astype(jnp.bfloat16)
        out_grads = []
        attended_grad = []
        for row in range(rows):
            span = slice(row * half_head, (row + 1) * half_head)
            out_grads.append(contract_rows(out_in, attended_low[:, span]))
            attended_grad.append(plain(out_in, mixing[row][:, 3 * half_head :]))
        attended_grad = jnp.concatenate(attended_grad, axis=1).astype(jnp.bfloat16)
        mixed_grad = [
            from_heads(part.astype(jnp.bfloat16))
            for part in attend_backward(*heads, document, logsum, by_heads(attended_grad))
        ]
        parts = []
        normed_grad = 0.0
        for row in range(rows):
            span = slice(row * half_head, (row + 1) * half_head)
            pieces = jnp.concatenate([part[:, span] for part in mixed_grad], axis=1)
            parts.append(
                jnp.concatenate([contract_rows(normed_one, pieces), out_grads[row]], axis=1)
            )
            normed_grad = normed_grad + contract_cols(pieces, mixing[row][:, : 3 * half_head])
        attention_grads[layer_at] = scatter_plane(parts)
        back_one, gain_one_grad, shift_one_grad = norm_backward(
            pair_sum(normed_grad), unit_one, inverse_one, gain_one
        )
        query_sums = jnp.stack(
            [jnp.sum(mixed_grad[part].astype(jnp.float32), axis=0) for part in (0, 2)]
        )
        vector_parts[layer_at] = (
            jnp.stack(
                [
                    gain_one_grad,
                    shift_one_grad,
                    jnp.sum(out_in.astype(jnp.float32), axis=0),
                    gain_two_grad,
                    shift_two_grad,
                    jnp.sum(down_in.astype(jnp.float32), axis=0),
                ]
            ),
            query_sums.reshape(2, rows, half_head),
            jnp.stack(hidden_grads),
        )
        gradient = middle_grad + back_one

    first_parts = [(attention_grads[layer], forward_grads[layer]) for layer in range(1, layers)]
    gradient, first_parts = lax.optimization_barrier((gradient, first_parts))
    for layer_at in range(1, layers):
        attention_grads[layer_at], forward_grads[layer_at] = first_parts[layer_at - 1]
    for layer_at in reversed(range(layers)):
        forward_grads[layer_at] = group_sum(forward_grads[layer_at])
        attention_grads[layer_at] = group_sum(attention_grads[layer_at])
    input_grad = to_owner(gradient)
    deep, asked, hidden = (
        jnp.stack([vector_parts[layer_at][part] for layer_at in range(layers)]) for part in range(3)
    )
    sums = vector_sum(
        jnp.concatenate([deep.reshape(-1), asked.reshape(-1), hidden.reshape(-1)])
    )
    ours = sums[deep.size :]
    hidden_sums = in_order("core", ours[None], swap(ours, "core")[None], 0)
    deep_sums = lax.dynamic_slice_in_dim(
        sums[: deep.size].reshape(layers, 6, width), (at_pair * 2 + at_core) * depth_in, depth_in, 2
    )
    asked_sums = hidden_sums[:, : asked.size].reshape(2, layers, 2, rows, half_head)
    asked_sums = lax.dynamic_index_in_dim(asked_sums, at_row, 3, keepdims=False)
    asked_sums = asked_sums.transpose(1, 2, 0, 3).reshape(layers, 2, head_width)
    up_sums = hidden_sums[:, asked.size :].reshape(2, layers, rows, half_hidden)
    up_sums = lax.dynamic_index_in_dim(up_sums, at_row, 2, keepdims=False)
    up_sums = up_sums.transpose(1, 0, 2).reshape(layers, hidden_width)

    attention_out = [return_weights(part) for part in attention_grads]
    forward_out = [return_weights(part) for part in forward_grads]
    split = 3 * half_head
    qkv_grad = jnp.stack([join_halves(part, 0, split, (3, half_head)) for part in attention_out])
    out_grad = jnp.stack(
        [join_halves(part, split, split + half_head, (half_head,)) for part in attention_out]
    )
    up_grad = jnp.stack([join_halves(part, 0, half_hidden, (half_hidden,)) for part in forward_out])
    down_grad = jnp.stack(
        [join_halves(part, half_hidden, 2 * half_hidden, (half_hidden,)) for part in forward_out]
    )
    return (
        activations,
        input_grad,
        deep_sums[:, 0],
        deep_sums[:, 1],
        qkv_grad,
        asked_sums,
        out_grad,
        deep_sums[:, 2],
        deep_sums[:, 3],
        deep_sums[:, 4],
        up_grad,
        up_sums,
        down_grad,
        deep_sums[:, 5],
    )


def solution(mesh):
    devices = mesh.devices
    depth, rows, cols = devices.shape
    chips = Mesh(devices.reshape(depth, rows, cols // 2, 2), ("dp", "row", "pair", "core"))
    col = ("pair", "core")
    placed = (
        P(col, ("dp", "row")),
        P(col, ("dp", "row")),
        P(("dp", "pair", "core"), None),
        P(None, col),
        P(None, col),
        P(None, col, None, "row"),
        P(None, None, "row"),
        P(None, col, "row"),
        P(None, col),
        P(None, col),
        P(None, col),
        P(None, col, "row"),
        P(None, "row"),
        P(None, col, "row"),
        P(None, col),
    )
    return jax.shard_map(
        shards,
        mesh=chips,
        in_specs=placed,
        out_specs=(
            P(col, ("dp", "row")),
            P(col, ("dp", "row")),
            P(None, col),
            P(None, col),
            P(None, col, None, "row"),
            P(None, None, "row"),
            P(None, col, "row"),
            P(None, col),
            P(None, col),
            P(None, col),
            P(None, col, "row"),
            P(None, "row"),
            P(None, col, "row"),
            P(None, col),
        ),
        check_vma=False,
    )
```
